32 devices in a mesh: band: 16 (over z, y, core), col: 2 (over x).
Axes of the slice: x: 2, y: 2, z: 4, core: 2. Of those that a mesh axis runs over, the one named last changes fastest.
Arguments:
- valence: bfloat16 [8, 64, 64, 128], P('col'), may hold values from -6 to 6
- conduction: bfloat16 [64, 64, 64, 128], P('band'), may hold values from -6 to 6
- energy_valence: float32 [8], P('col'), may hold values from -6 to -1
- energy_conduction: float32 [64], P('band'), may hold values from 0.5 to 6
- occ_valence: int32 [8], P('col'), may hold values from 1 to 2
- occ_conduction: int32 [64], P('band'), may hold values from 0 to 1
- gvec_index: int32 [10240], replicated, may hold values from 0 to 262143, as said below
Outputs:
- chi_zero: float32 [2, 10240, 10240], P(None, 'band', 'col')
The draws below stay inside these ranges and needn't reach their ends.
Inputs may be any that keep to these rules, and one draw needn't show every extreme that they name: `gvec_index`: distinct indices of the 10240 grid points with the shortest wave vectors, where index x * 64 * 64 + y * 64 + z stands for the vector with components ((x + 32) mod 64) - 32 and so on; ordered by length, equal lengths in any order.
All inputs are finite; a program needn't handle non-finite values.
Results may differ from the reference program's by a relative error of at most 0.01.
Values may be sent and summed in bfloat16 or wider, within the bound.
A program may use at most 320 MiB of HBM per device.

```python
import math
import jax
import jax.numpy as jnp
from jax import lax

NG = 64
NPW = 10240
NV = 8
NC = 64


def draw_gvec_index(key, part):
    key = jax.random.fold_in(key, 11)
    total = NG * NG * NG
    flat = jnp.arange(total, dtype=jnp.int32)
    half = NG // 2
    comp_x = (flat // (NG * NG) + half) % NG - half
    comp_y = (flat // NG % NG + half) % NG - half
    comp_z = (flat % NG + half) % NG - half
    length = comp_x * comp_x + comp_y * comp_y + comp_z * comp_z
    tiebreak = jax.random.permutation(key, total).astype(jnp.int32)
    score = length * total + tiebreak
    order = jnp.argsort(score, stable=True).astype(jnp.int32)
    return order[:NPW]


def plant(array, key, least, high):
    spot = [jax.random.randint(jax.random.fold_in(key, axis), (), 0, length) for axis, length in enumerate(array.shape)]
    main_axis = array.shape.index(max(array.shape))
    neighbour = spot[:main_axis] + [(spot[main_axis] + 1) % array.shape[main_axis]] + spot[main_axis + 1:]
    return array.at[tuple(spot)].set(least).at[tuple(neighbour)].set(high)


def block_scale(own_key, shape, split, smallest, top_value):
    def one(dim, parts):
        draws = jax.random.uniform(jax.random.fold_in(jax.random.fold_in(own_key, 6), dim), (parts,), jnp.float32, smallest / len(split), top_value / len(split))
        return jnp.repeat(jnp.exp(draws), shape[dim] // parts).reshape((-1,) + (1,) * (len(shape) - dim - 1))

    gain = one(*split[0])
    for cut in split[1:]:
        gain = gain * one(*cut)
    return gain


def normal_values(stream_key, extent, scale, limit, split=(), kind=jnp.bfloat16):
    loudness = block_scale(stream_key, extent, split, -0.22, 0.18) if split else 1.0
    drawn = jax.random.normal(stream_key, extent, jnp.float32) * scale * loudness
    return jnp.minimum(jnp.maximum(drawn, -limit), limit).astype(kind)


def setup_inputs(seed: int = 0) -> dict:
    splits = jax.random.split(jax.random.key(seed), 8)
    return {
        "valence": normal_values(splits[0], (NV, NG, NG, 2 * NG), 1.0, 6.0, ((0, 2),)),
        "conduction": normal_values(splits[1], (NC, NG, NG, 2 * NG), 1.0, 6.0, ((0, 16),)),
        "energy_valence": jnp.clip(-6.0 + 5.0 * jax.random.uniform(splits[2], (NV,), jnp.float32) ** block_scale(splits[2], (NV,), ((0, 2),), -0.2, 0.2), -6.0, -1.0),
        "energy_conduction": jnp.clip(0.5 + 5.5 * jax.random.uniform(splits[3], (NC,), jnp.float32) ** block_scale(splits[3], (NC,), ((0, 16),), -0.2, 0.2), 0.5, 6.0),
        "occ_valence": plant(jax.random.randint(splits[4], (NV,), 1, 3), jax.random.fold_in(splits[4], 1), 1, 2).astype(jnp.int32),
        "occ_conduction": plant(jax.random.randint(splits[5], (NC,), 0, 2), jax.random.fold_in(splits[5], 1), 0, 1).astype(jnp.int32),
        "gvec_index": draw_gvec_index(jax.random.fold_in(splits[7], 71), 0),
    }


def dft_table():
    freq = jnp.arange(NG, dtype=jnp.int32)
    product = freq[:, None] * freq[None, :] % NG
    angle = 2.0 * math.pi / NG * product.astype(jnp.float32)
    cosine = jnp.cos(angle) / math.sqrt(NG)
    sine = jnp.sin(angle) / math.sqrt(NG)
    table = jnp.stack([jnp.stack([cosine, sine]), jnp.stack([-sine, cosine])])
    return table.astype(jnp.bfloat16)

def transform(field, table, form):
    return jnp.einsum(form, table.astype(jnp.float32), field.astype(jnp.float32)).astype(jnp.bfloat16)

def reference(valence, conduction, energy_valence, energy_conduction, occ_valence, occ_conduction, gvec_index):
    table = dft_table()
    val_grid = jnp.transpose(valence.reshape(NV, NG, NG, 2, NG), (0, 3, 1, 2, 4)).reshape(NV, 2, NG, NG * NG)
    val_re = val_grid[:, 0].astype(jnp.float32)
    val_im = val_grid[:, 1].astype(jnp.float32)

    def one_band(cond_band):
        cond_grid = jnp.transpose(cond_band.reshape(NG, NG, 2, NG), (2, 0, 1, 3)).reshape(2, NG, NG * NG)
        cond_re = cond_grid[0].astype(jnp.float32)
        cond_im = cond_grid[1].astype(jnp.float32)
        real_part = val_re * cond_re + val_im * cond_im
        imag_part = val_re * cond_im - val_im * cond_re
        field = jnp.stack([real_part, imag_part], axis=1).astype(jnp.bfloat16)
        field = field.reshape(NV, 2, NG, NG, NG)
        field = transform(field, table, 'oikx,vixyz->vokyz')
        field = transform(field, table, 'oiky,vixyz->voxkz')
        field = transform(field, table, 'oikz,vixyz->voxyk')
        flat = field.reshape(NV, 2, NG * NG * NG)
        return jnp.take(flat, gvec_index, axis=2)
    rho = lax.map(one_band, conduction)
    rho = jnp.transpose(rho, (1, 0, 2, 3))
    count = conduction.shape[0]
    occ_diff = (occ_valence[:, None] - occ_conduction[None, :]).astype(jnp.float32)
    weight = occ_diff / (energy_valence[:, None] - energy_conduction[None, :]) / math.sqrt(NV * count)
    weighted = (weight[:, :, None, None] * rho.astype(jnp.float32)).astype(jnp.bfloat16)
    rotated = jnp.stack([-rho[:, :, 1], rho[:, :, 0]], axis=2)
    columns = jnp.concatenate([rho, rotated], axis=3)
    tile = lax.dot_general(weighted.astype(jnp.float32), columns.astype(jnp.float32), (((0, 1, 2), (0, 1, 2)), ((), ())), preferred_element_type=jnp.float32)
    npw = rho.shape[3]
    return jnp.transpose(tile.reshape(npw, 2, npw), (1, 0, 2))
```

```python
import functools
import math

import jax
import jax.numpy as jnp
import ml_dtypes
import numpy as np
from jax import lax
from jax.experimental import pallas as pl
from jax.experimental.pallas import tpu as pltpu
from jax.sharding import PartitionSpec as P

PAD = 32
VMEM = 56 * 1024 * 1024


def sphere(grid, count):
    comp = (np.arange(grid) + grid // 2) % grid - grid // 2
    square = comp * comp
    lengths = square[:, None, None] + square[None, :, None] + square[None, None, :]
    top = int(np.sort(lengths.ravel())[count - 1])
    reach = math.isqrt(top)
    widths = [2 * math.isqrt(top - k * k) + 1 for k in range(-reach, reach + 1)]
    offsets = [0]
    for width in widths:
        offsets.append(offsets[-1] + width)
    return reach, offsets


def tables(grid, reach):
    freq = np.arange(PAD) - reach
    kept = (np.arange(PAD) < 2 * reach + 1).astype(np.float64)
    rank = np.arange(PAD)
    ranked = (rank + 1) // 2 * np.where(rank % 2 == 1, 1, -1)

    def pair(values):
        angle = 2.0 * math.pi / grid * ((values[:, None] * np.arange(grid)[None, :]) % grid)
        return (
            np.cos(angle) / math.sqrt(grid) * kept[:, None],
            np.sin(angle) / math.sqrt(grid) * kept[:, None],
        )

    cosine, sine = pair(freq)
    full = np.array([[cosine, sine], [-sine, cosine]])
    swapped = np.array([full[1], -full[0]])
    z_block = np.zeros((2, 2, grid, 2, PAD, 2, 2))
    for member in range(2):
        for which, part in enumerate((full, swapped)):
            z_block[member, :, :, which, :, member, :] = np.transpose(part, (1, 3, 2, 0))
    z_matrix = z_block.reshape(4 * grid, 8 * PAD)
    one = np.array([[cosine, sine], [-sine, cosine]])
    y_block = np.zeros((2, 2, PAD, 2, 2, grid))
    for member in range(2):
        y_block[member, :, :, member] = np.transpose(one, (0, 2, 1, 3))
    y_matrix = y_block.reshape(4 * PAD, 4 * grid)
    cos_x, sin_x = pair(ranked)
    x_block = np.zeros((2, PAD, 2, grid, 2))
    for member in range(2):
        x_block[member, :, member] = np.stack([cos_x, sin_x], axis=-1)
    x_matrix = x_block.reshape(2 * PAD, 4 * grid)
    return [m.astype(ml_dtypes.bfloat16) for m in (z_matrix, y_matrix, x_matrix)]


def transform_kernel(
    grid, offsets, packed, val_ref, cond_ref, z_ref, y_ref, x_ref, out_ref, mid, cols
):
    half = 2 * PAD * 2
    lane = lax.broadcasted_iota(jnp.int32, (2 * grid, 2 * grid), 1)
    low = lane < grid

    def planes(step, carry):
        val = val_ref[0, pl.ds(step * 2, 2)].reshape(2 * grid, 2 * grid).astype(jnp.float32)
        turned = pltpu.roll(val, grid, 1)
        val_re = jnp.where(low, val, turned)
        val_im = jnp.where(low, turned, -val)
        fields = []
        for band in range(4):
            cond = cond_ref[band, pl.ds(step * 2, 2)].reshape(2 * grid, 2 * grid)
            cond = cond.astype(jnp.float32)
            product = val_re * cond + val_im * pltpu.roll(cond, grid, 1)
            fields.append(product.astype(jnp.bfloat16))
        parts = []
        for first in (0, 2):
            both = jnp.concatenate(fields[first : first + 2], axis=1)
            parts.append(
                jnp.dot(both, z_ref[...], preferred_element_type=jnp.float32).astype(jnp.bfloat16)
            )
        stacked = []
        for plane in range(2):
            rows = slice(plane * grid, (plane + 1) * grid)
            for which in range(2):
                lanes = slice(which * half, (which + 1) * half)
                stacked.append(
                    jnp.concatenate([parts[0][rows, lanes], parts[1][rows, lanes]], axis=1)
                )
        stacked = jnp.concatenate(stacked, axis=0)
        found = jnp.dot(y_ref[...], stacked, preferred_element_type=jnp.float32)
        start = pl.multiple_of(step * 4 * PAD, 4 * PAD)
        for side in range(2):
            mid[side, pl.ds(start, 4 * PAD), :] = found[:, side * half : (side + 1) * half]
        return carry

    lax.fori_loop(0, grid // 2, planes, 0)
    cols[...] = jnp.zeros_like(cols)
    count = len(offsets) - 1
    for first in range(0, count, 2):
        rows = [
            jnp.concatenate(
                [
                    mid[side, pl.ds(first + member, 2 * grid, stride=PAD), :].astype(jnp.bfloat16)
                    for side in range(2)
                ],
                axis=1,
            )
            for member in range(2)
        ]
        found = jnp.dot(
            x_ref[...], jnp.concatenate(rows, axis=0), preferred_element_type=jnp.float32
        )
        for member in range(2):
            if first + member < count:
                start = offsets[first + member]
                cols[start : start + PAD, :] = found[member * PAD : (member + 1) * PAD]
    turned = cols[...].T
    for k in range(PAD):
        out_ref[k, 0:4, :] = turned[4 * k : 4 * k + 4]
        out_ref[k, 4:8, :] = turned[half + 4 * k : half + 4 * k + 4]


def pick_kernel(count, rows, packed, field_ref, col_ref, sel_ref, out_ref, held):
    @pl.when(pl.program_id(0) == 0)
    def _():
        held[...] = field_ref[0:count].reshape(count * rows, packed).astype(jnp.bfloat16)

    tile = out_ref.shape[1]
    place = lax.broadcasted_iota(jnp.int32, (packed, tile), 0)
    chosen = jnp.where(place == col_ref[...], 1.0, 0.0).astype(jnp.bfloat16)
    found = jnp.dot(held[...], chosen, preferred_element_type=jnp.float32)
    select = jnp.broadcast_to(sel_ref[...], (rows, tile))
    total = jnp.zeros((rows, tile), jnp.float32)
    for k in range(count):
        total = total + jnp.where(select == k, found[k * rows : (k + 1) * rows], 0.0)
    out_ref[...] = total.astype(jnp.bfloat16)


def densities(valence, conduction, gvec_index):
    val_local, grid = valence.shape[0], valence.shape[1]
    npw = gvec_index.shape[0]
    reach, offsets = sphere(grid, npw)
    count = 2 * reach + 1
    assert count <= PAD and conduction.shape[0] == 4
    packed = -(-(offsets[-2] + PAD) // 128) * 128
    z_matrix, y_matrix, x_matrix = tables(grid, reach)
    features = 8 * val_local
    whole = lambda shape: pl.BlockSpec(shape, lambda v: (0,) * len(shape))
    field = pl.pallas_call(
        functools.partial(transform_kernel, grid, offsets, packed),
        grid=(val_local,),
        in_specs=[
            pl.BlockSpec((1, grid, grid, 2 * grid), lambda v: (v, 0, 0, 0)),
            whole(conduction.shape),
            whole(z_matrix.shape),
            whole(y_matrix.shape),
            whole(x_matrix.shape),
        ],
        out_specs=pl.BlockSpec((PAD, 8, packed), lambda v: (0, v, 0)),
        out_shape=jax.ShapeDtypeStruct((PAD, features, packed), jnp.float32),
        scratch_shapes=[
            pltpu.VMEM((2, 2 * grid * PAD, 4 * PAD), jnp.float32),
            pltpu.VMEM((packed, 8 * PAD), jnp.float32),
        ],
        compiler_params=pltpu.CompilerParams(vmem_limit_bytes=VMEM),
        name="transform",
    )(valence, conduction, z_matrix, y_matrix, x_matrix)

    half = grid // 2
    wrap = lambda part: (part + half) % grid - half
    x_comp = wrap(gvec_index // (grid * grid))
    y_comp = wrap(gvec_index // grid % grid)
    z_comp = wrap(gvec_index % grid)
    col = jnp.where(x_comp > 0, 2 * x_comp - 1, -2 * x_comp)
    for k in range(count):
        col = col + jnp.where(y_comp == k - reach, offsets[k], 0)
    tile = 256
    return pl.pallas_call(
        functools.partial(pick_kernel, count, features, packed),
        grid=(npw // tile,),
        in_specs=[
            whole((PAD, features, packed)),
            pl.BlockSpec((1, tile), lambda g: (0, g)),
            pl.BlockSpec((1, tile), lambda g: (0, g)),
        ],
        out_specs=pl.BlockSpec((features, tile), lambda g: (0, g)),
        out_shape=jax.ShapeDtypeStruct((features, npw), jnp.bfloat16),
        scratch_shapes=[pltpu.VMEM((count * features, packed), jnp.bfloat16)],
        compiler_params=pltpu.CompilerParams(vmem_limit_bytes=VMEM),
        name="pick",
    )(field, col[None], (z_comp + reach)[None])


def pair_weights(energy_valence, energy_conduction, occ_valence, occ_conduction):
    total_val = energy_valence.shape[0] * lax.axis_size("col")
    total_cond = energy_conduction.shape[0] * lax.axis_size("band")
    occ_diff = (occ_valence[:, None] - occ_conduction[None, :]).astype(jnp.float32)
    return (
        occ_diff
        / (energy_valence[:, None] - energy_conduction[None, :])
        / math.sqrt(total_val * total_cond)
    )


def local(
    valence, conduction, energy_valence, energy_conduction, occ_valence, occ_conduction, gvec_index
):
    rho = densities(valence, conduction, gvec_index)
    features, npw = rho.shape
    weight = pair_weights(energy_valence, energy_conduction, occ_valence, occ_conduction)
    weight = jnp.repeat(weight.reshape(-1), 2)
    weighted = (weight[:, None] * rho.astype(jnp.float32)).astype(jnp.bfloat16)
    cols = lax.all_to_all(rho, "col", split_axis=1, concat_axis=0, tiled=True)
    cols = lax.all_gather(cols, "band", axis=0, tiled=True)
    rows = lax.all_to_all(weighted, "band", split_axis=1, concat_axis=0, tiled=True)
    rows = lax.all_gather(rows, "col", axis=0, tiled=False)
    n_col, n_band = lax.axis_size("col"), lax.axis_size("band")
    rows = rows.reshape(n_col, n_band, features // 2, 2, npw // n_band)
    rows = jnp.transpose(rows, (1, 0, 2, 3, 4))
    turned = jnp.stack([rows[:, :, :, 1], -rows[:, :, :, 0]], axis=3)
    depth = n_col * n_band * features
    both = jnp.concatenate(
        [rows.reshape(depth, npw // n_band), turned.reshape(depth, npw // n_band)], axis=1
    )
    tile = lax.dot_general(
        both, cols, (((0,), (0,)), ((), ())), preferred_element_type=jnp.float32
    )
    return tile.reshape(2, npw // n_band, cols.shape[1])


def solution(mesh):
    return jax.shard_map(
        local,
        mesh=mesh,
        in_specs=(
            P("col", None, None, None),
            P("band", None, None, None),
            P("col"),
            P("band"),
            P("col"),
            P("band"),
            P(),
        ),
        out_specs=P(None, "band", "col"),
        check_vma=False,
    )
```

```python
import functools
import math

import jax
import jax.numpy as jnp
import ml_dtypes
import numpy as np
from jax import lax
from jax.experimental import pallas as pl
from jax.experimental.pallas import tpu as pltpu
from jax.sharding import PartitionSpec as P

PAD = 32
VMEM = 56 * 1024 * 1024


def sphere(grid, count):
    comp = (np.arange(grid) + grid // 2) % grid - grid // 2
    square = comp * comp
    lengths = square[:, None, None] + square[None, :, None] + square[None, None, :]
    top = int(np.sort(lengths.ravel())[count - 1])
    reach = math.isqrt(top)
    widths = [2 * math.isqrt(top - k * k) + 1 for k in range(-reach, reach + 1)]
    offsets = [0]
    for width in widths:
        offsets.append(offsets[-1] + width)
    return reach, offsets


def tables(grid, reach):
    freq = np.arange(PAD) - reach
    kept = (np.arange(PAD) < 2 * reach + 1).astype(np.float64)
    rank = np.arange(PAD)
    ranked = (rank + 1) // 2 * np.where(rank % 2 == 1, 1, -1)

    def pair(values):
        angle = 2.0 * math.pi / grid * ((values[:, None] * np.arange(grid)[None, :]) % grid)
        return (
            np.cos(angle) / math.sqrt(grid) * kept[:, None],
            np.sin(angle) / math.sqrt(grid) * kept[:, None],
        )

    cosine, sine = pair(freq)
    full = np.array([[cosine, sine], [-sine, cosine]])
    swapped = np.array([full[1], -full[0]])
    z_block = np.zeros((2, 2, grid, 2, PAD, 2, 2))
    for member in range(2):
        for which, part in enumerate((full, swapped)):
            z_block[member, :, :, which, :, member, :] = np.transpose(part, (1, 3, 2, 0))
    z_matrix = z_block.reshape(4 * grid, 8 * PAD)
    one = np.array([[cosine, sine], [-sine, cosine]])
    y_block = np.zeros((2, 2, PAD, 2, 2, grid))
    for member in range(2):
        y_block[member, :, :, member] = np.transpose(one, (0, 2, 1, 3))
    y_matrix = y_block.reshape(4 * PAD, 4 * grid)
    cos_x, sin_x = pair(ranked)
    x_block = np.zeros((2, PAD, 2, grid, 2))
    for member in range(2):
        x_block[member, :, member] = np.stack([cos_x, sin_x], axis=-1)
    x_matrix = x_block.reshape(2 * PAD, 4 * grid)
    return [m.astype(ml_dtypes.bfloat16) for m in (z_matrix, y_matrix, x_matrix)]


def transform_kernel(
    grid, offsets, packed, val_ref, cond_ref, z_ref, y_ref, x_ref, out_ref, mid, cols
):
    half = 2 * PAD * 2
    lane = lax.broadcasted_iota(jnp.int32, (2 * grid, 2 * grid), 1)
    low = lane < grid

    def planes(step, carry):
        val = val_ref[0, pl.ds(step * 2, 2)].reshape(2 * grid, 2 * grid).astype(jnp.float32)
        turned = pltpu.roll(val, grid, 1)
        val_re = jnp.where(low, val, turned)
        val_im = jnp.where(low, turned, -val)
        fields = []
        for band in range(4):
            cond = cond_ref[band, pl.ds(step * 2, 2)].reshape(2 * grid, 2 * grid)
            cond = cond.astype(jnp.float32)
            product = val_re * cond + val_im * pltpu.roll(cond, grid, 1)
            fields.append(product.astype(jnp.bfloat16))
        parts = []
        for first in (0, 2):
            both = jnp.concatenate(fields[first : first + 2], axis=1)
            parts.append(
                jnp.dot(both, z_ref[...], preferred_element_type=jnp.float32).astype(jnp.bfloat16)
            )
        stacked = []
        for plane in range(2):
            rows = slice(plane * grid, (plane + 1) * grid)
            for which in range(2):
                lanes = slice(which * half, (which + 1) * half)
                stacked.append(
                    jnp.concatenate([parts[0][rows, lanes], parts[1][rows, lanes]], axis=1)
                )
        stacked = jnp.concatenate(stacked, axis=0)
        found = jnp.dot(y_ref[...], stacked, preferred_element_type=jnp.float32)
        start = pl.multiple_of(step * 4 * PAD, 4 * PAD)
        for side in range(2):
            mid[side, pl.ds(start, 4 * PAD), :] = found[:, side * half : (side + 1) * half]
        return carry

    lax.fori_loop(0, grid // 2, planes, 0)
    cols[...] = jnp.zeros_like(cols)
    count = len(offsets) - 1
    for first in range(0, count, 2):
        rows = [
            jnp.concatenate(
                [
                    mid[side, pl.ds(first + member, 2 * grid, stride=PAD), :].astype(jnp.bfloat16)
                    for side in range(2)
                ],
                axis=1,
            )
            for member in range(2)
        ]
        found = jnp.dot(
            x_ref[...], jnp.concatenate(rows, axis=0), preferred_element_type=jnp.float32
        )
        for member in range(2):
            if first + member < count:
                start = offsets[first + member]
                cols[start : start + PAD, :] = found[member * PAD : (member + 1) * PAD]
    turned = cols[...].T
    for k in range(PAD):
        out_ref[k, 0:4, :] = turned[4 * k : 4 * k + 4]
        out_ref[k, 4:8, :] = turned[half + 4 * k : half + 4 * k + 4]


def pick_tile(count, rows, packed, held, col, sel):
    tile = col.shape[1]
    place = lax.broadcasted_iota(jnp.int32, (packed, tile), 0)
    chosen = jnp.where(place == col, 1.0, 0.0).astype(jnp.bfloat16)
    found = jnp.dot(held[...], chosen, preferred_element_type=jnp.float32)
    select = jnp.broadcast_to(sel, (rows, tile))
    total = jnp.zeros((rows, tile), jnp.float32)
    for k in range(count):
        total = total + jnp.where(select == k, found[k * rows : (k + 1) * rows], 0.0)
    return total.astype(jnp.bfloat16)


def gather_kernel(
    plan, field_ref, col_ref, sel_ref, all_ref, row_ref, held, stage,
    x_send, x_recv, x_local, send, recv, r_send, r_recv, r_local,
):
    count, rows, packed, n_band, n_col, chunks, width, tile, share, window = plan
    n_z = n_band // 4
    me = lax.axis_index("band")
    my_col = lax.axis_index("col")
    z, y, core = me // 4, me // 2 % 2, me % 2
    y_peer = z * 4 + (1 - y) * 2 + core
    core_peer = z * 4 + y * 2 + 1 - core
    span = chunks * width

    def remote(src, dst, send_sem, recv_sem, **target):
        return pltpu.make_async_remote_copy(
            src_ref=src,
            dst_ref=dst,
            send_sem=send_sem,
            recv_sem=recv_sem,
            device_id=target,
            device_id_type=pl.DeviceIdType.MESH,
        )

    def inside(value):
        return (value >= 0) & (value < n_z)

    barrier = pltpu.get_barrier_semaphore()

    def greet(**target):
        pl.semaphore_signal(
            barrier, inc=1, device_id=target, device_id_type=pl.DeviceIdType.MESH
        )

    for step in (1, -1):
        pl.when(inside(z + step))(functools.partial(greet, band=me + 4 * step))
    greet(band=y_peer)
    greet(band=core_peer)
    for p in range(1, n_col):
        greet(col=(my_col + p) % n_col)
    known = (z > 0).astype(jnp.int32) + (z < n_z - 1).astype(jnp.int32) + 1 + n_col
    pl.semaphore_wait(barrier, known)

    held[...] = field_ref[0:count].reshape(count * rows, packed).astype(jnp.bfloat16)

    def lanes(j):
        return pl.ds(pl.multiple_of(j * width, 128), width)

    def block(slot, j):
        return all_ref.at[slot, :, :, lanes(j)]

    def relay(slot, j, kind, target):
        view = block(slot, j)
        return remote(view, view, send.at[j, kind, slot], recv.at[j, slot], band=target)

    def staged(j, owner):
        return stage.at[:, pl.ds(pl.multiple_of(owner * span + j * width, 128), width)]

    def across(j, p):
        peer = (my_col + p) % n_col
        return remote(
            staged(j, peer),
            all_ref.at[me, my_col, :, lanes(j)],
            x_send.at[j, p],
            x_recv.at[j, p],
            col=peer,
        )

    def own(j):
        return pltpu.make_async_copy(
            staged(j, my_col), all_ref.at[me, my_col, :, lanes(j)], x_local.at[j]
        )

    def pick(j):
        per = width // tile

        def body(i, carry):
            start = pl.multiple_of((i // per) * span + j * width + (i % per) * tile, 128)
            where = pl.ds(start, tile)
            stage[:, where] = pick_tile(
                count, rows, packed, held, col_ref[:, where], sel_ref[:, where]
            )
            return carry

        lax.fori_loop(0, n_col * per, body, 0)
        own(j).start()
        for p in range(1, n_col):
            across(j, p).start()

    def along_z(j, h, act):
        if h == 0 and act == "start":
            own(j).wait()
            for p in range(1, n_col):
                across(j, p).wait_recv()
        for step in (1, -1):
            source = z - step * h
            slot = source * 4 + y * 2 + core

            @pl.when(inside(source))
            def _():
                if h > 0 and act == "start":
                    relay(slot, j, 2, y_peer).wait_recv()

                @pl.when(inside(z + step))
                def _():
                    getattr(relay(slot, j, 0 if step == 1 else 1, me + 4 * step), act)()

                if h > 0 or step == 1:
                    getattr(relay(slot, j, 2, y_peer), act)()
                    getattr(relay(slot, j, 3, core_peer), act)()

    def along_y(j, h, act):
        for step in (1, -1) if h > 0 else (1,):
            source = z - step * h
            slot = source * 4 + (1 - y) * 2 + core

            @pl.when(inside(source))
            def _():
                copy = relay(slot, j, 3, core_peer)
                if act == "start":
                    copy.wait_recv()
                getattr(copy, act)()

    per_col = n_band // n_col
    owner = me // per_col
    base = me % per_col * share // 128 * 128

    def row_copy(i, p):
        return remote(
            all_ref.at[:, :, :, pl.ds(pl.multiple_of(base + 128 * i, 128), 128)],
            row_ref.at[:, :, :, pl.ds(128 * i, 128)],
            r_send.at[i, p],
            r_recv.at[i],
            col=(my_col + p) % n_col,
        )

    def row_local(i):
        return pltpu.make_async_copy(
            all_ref.at[:, :, :, pl.ds(pl.multiple_of(base + 128 * i, 128), 128)],
            row_ref.at[:, :, :, pl.ds(128 * i, 128)],
            r_local.at[i],
        )

    def finish(j):
        for other in range(2 * n_z):
            slot = other * 2 + 1 - core
            relay(slot, j, 3, core_peer).wait_recv()
        for i in range(window // 128):

            @pl.when((owner == my_col) & ((base + 128 * i) // width == j))
            def _():
                row_local(i).start()
                for p in range(1, n_col):
                    row_copy(i, p).start()

    def tick(t, carry):
        def at(lag, act):
            j = t - lag
            pl.when((j >= 0) & (j < chunks))(lambda: act(j))

        at(0, pick)
        at(n_z + 2, finish)
        for h in range(n_z - 1, -1, -1):
            at(2 + h, lambda j: along_y(j, h, "start"))
            at(1 + h, lambda j: along_z(j, h, "start"))
        return carry

    lax.fori_loop(0, chunks + n_z + 2, tick, 0)

    def settle(j, carry):
        for p in range(1, n_col):
            across(j, p).wait_send()
        for h in range(n_z):
            along_z(j, h, "wait_send")
            along_y(j, h, "wait_send")
        return carry

    lax.fori_loop(0, chunks, settle, 0)
    for i in range(window // 128):

        @pl.when(owner == my_col)
        def _():
            row_local(i).wait()
            for p in range(1, n_col):
                row_copy(i, p).wait_send()

        @pl.when(owner != my_col)
        def _():
            row_copy(i, 1).wait_recv()


def densities(valence, conduction, gvec_index):
    val_local, grid = valence.shape[0], valence.shape[1]
    npw = gvec_index.shape[0]
    reach, offsets = sphere(grid, npw)
    count = 2 * reach + 1
    assert count <= PAD and conduction.shape[0] == 4
    packed = -(-(offsets[-2] + PAD) // 128) * 128
    z_matrix, y_matrix, x_matrix = tables(grid, reach)
    features = 8 * val_local
    whole = lambda shape: pl.BlockSpec(shape, lambda v: (0,) * len(shape))
    field = pl.pallas_call(
        functools.partial(transform_kernel, grid, offsets, packed),
        grid=(val_local,),
        in_specs=[
            pl.BlockSpec((1, grid, grid, 2 * grid), lambda v: (v, 0, 0, 0)),
            whole(conduction.shape),
            whole(z_matrix.shape),
            whole(y_matrix.shape),
            whole(x_matrix.shape),
        ],
        out_specs=pl.BlockSpec((PAD, 8, packed), lambda v: (0, v, 0)),
        out_shape=jax.ShapeDtypeStruct((PAD, features, packed), jnp.float32),
        scratch_shapes=[
            pltpu.VMEM((2, 2 * grid * PAD, 4 * PAD), jnp.float32),
            pltpu.VMEM((packed, 8 * PAD), jnp.float32),
        ],
        compiler_params=pltpu.CompilerParams(vmem_limit_bytes=VMEM),
        name="transform",
    )(valence, conduction, z_matrix, y_matrix, x_matrix)

    half = grid // 2
    wrap = lambda part: (part + half) % grid - half
    x_comp = wrap(gvec_index // (grid * grid))
    y_comp = wrap(gvec_index // grid % grid)
    z_comp = wrap(gvec_index % grid)
    col = jnp.where(x_comp > 0, 2 * x_comp - 1, -2 * x_comp)
    for k in range(count):
        col = col + jnp.where(y_comp == k - reach, offsets[k], 0)
    return field, col[None], (z_comp + reach)[None], count, packed


def gathered(field, col, sel, count, packed):
    features, npw = field.shape[1], col.shape[1]
    n_band, n_col = lax.axis_size("band"), lax.axis_size("col")
    chunks = 5
    width = npw // n_col // chunks
    tile = min(512, width)
    share = npw // n_band
    window = -(-share // 128) * 128
    assert window >= share + max(share * r % 128 for r in range(n_band // n_col))
    plan = (count, features, packed, n_band, n_col, chunks, width, tile, share, window)
    vmem = pl.BlockSpec(memory_space=pltpu.VMEM)
    dma = pltpu.SemaphoreType.DMA
    pieces = window // 128
    cols, rows = pl.pallas_call(
        functools.partial(gather_kernel, plan),
        in_specs=[vmem] * 3,
        out_specs=[pl.BlockSpec(memory_space=pl.ANY)] * 2,
        out_shape=[
            jax.ShapeDtypeStruct((n_band, n_col, features, chunks * width), jnp.bfloat16),
            jax.ShapeDtypeStruct((n_band, n_col, features, window), jnp.bfloat16),
        ],
        scratch_shapes=[
            pltpu.VMEM((count * features, packed), jnp.bfloat16),
            pltpu.VMEM((features, npw), jnp.bfloat16),
            dma((chunks, n_col)),
            dma((chunks, n_col)),
            dma((chunks,)),
            dma((chunks, 4, n_band)),
            dma((chunks, n_band)),
            dma((pieces, n_col)),
            dma((pieces,)),
            dma((pieces,)),
        ],
        compiler_params=pltpu.CompilerParams(
            vmem_limit_bytes=VMEM, collective_id=0, has_side_effects=True
        ),
        name="pick_and_gather",
    )(field, col, sel)
    if share % 128:
        start = lax.axis_index("band") % (n_band // n_col) * share % 128
        rows = lax.dynamic_slice_in_dim(rows, start, share, axis=3)
    return cols, rows


def pair_weights(energy_valence, energy_conduction, occ_valence, occ_conduction):
    total_val = energy_valence.shape[0] * lax.axis_size("col")
    total_cond = energy_conduction.shape[0] * lax.axis_size("band")
    occ_diff = (occ_valence[:, None] - occ_conduction[None, :]).astype(jnp.float32)
    return (
        occ_diff
        / (energy_valence[:, None] - energy_conduction[None, :])
        / math.sqrt(total_val * total_cond)
    )


def local(
    valence, conduction, energy_valence, energy_conduction, occ_valence, occ_conduction, gvec_index
):
    weight = pair_weights(energy_valence, energy_conduction, occ_valence, occ_conduction)
    weight = lax.all_gather(weight.reshape(-1), ("band", "col"), axis=0, tiled=False)
    cols, rows = gathered(*densities(valence, conduction, gvec_index))
    n_band, n_col, features, share = rows.shape
    depth = n_band * n_col * features
    rows = rows.reshape(depth // 2, 2, share).astype(jnp.float32)
    rows = (weight.reshape(-1)[:, None, None] * rows).astype(jnp.bfloat16)
    turned = jnp.stack([rows[:, 1], -rows[:, 0]], axis=1)
    both = jnp.concatenate([rows.reshape(depth, share), turned.reshape(depth, share)], axis=1)
    tile = lax.dot_general(
        both,
        cols.reshape(depth, -1),
        (((0,), (0,)), ((), ())),
        preferred_element_type=jnp.float32,
    )
    return tile.reshape(2, share, cols.shape[3])


def solution(mesh):
    return jax.shard_map(
        local,
        mesh=mesh,
        in_specs=(
            P("col", None, None, None),
            P("band", None, None, None),
            P("col"),
            P("band"),
            P("col"),
            P("band"),
            P(),
        ),
        out_specs=P(None, "band", "col"),
        check_vma=False,
    )
```

```python
import functools
import math

import jax
import jax.numpy as jnp
import ml_dtypes
import numpy as np
from jax import lax
from jax.experimental import pallas as pl
from jax.experimental.pallas import tpu as pltpu
from jax.sharding import PartitionSpec as P

PAD = 32
VMEM = 56 * 1024 * 1024


def sphere(grid, count):
    comp = (np.arange(grid) + grid // 2) % grid - grid // 2
    square = comp * comp
    lengths = square[:, None, None] + square[None, :, None] + square[None, None, :]
    top = int(np.sort(lengths.ravel())[count - 1])
    reach = math.isqrt(top)
    widths = [2 * math.isqrt(top - k * k) + 1 for k in range(-reach, reach + 1)]
    offsets = [0]
    for width in widths:
        offsets.append(offsets[-1] + width)
    return reach, offsets


def tables(grid, reach):
    freq = np.arange(PAD) - reach
    kept = (np.arange(PAD) < 2 * reach + 1).astype(np.float64)
    rank = np.arange(PAD)
    ranked = (rank + 1) // 2 * np.where(rank % 2 == 1, 1, -1)

    def pair(values):
        angle = 2.0 * math.pi / grid * ((values[:, None] * np.arange(grid)[None, :]) % grid)
        return (
            np.cos(angle) / math.sqrt(grid) * kept[:, None],
            np.sin(angle) / math.sqrt(grid) * kept[:, None],
        )

    cosine, sine = pair(freq)
    full = np.array([[cosine, sine], [-sine, cosine]])
    swapped = np.array([full[1], -full[0]])
    z_block = np.zeros((2, 2, grid, 2, PAD, 2, 2))
    for member in range(2):
        for which, part in enumerate((full, swapped)):
            z_block[member, :, :, which, :, member, :] = np.transpose(part, (1, 3, 2, 0))
    z_matrix = z_block.reshape(4 * grid, 8 * PAD)
    one = np.array([[cosine, sine], [-sine, cosine]])
    y_block = np.zeros((2, 2, PAD, 2, 2, grid))
    for member in range(2):
        y_block[member, :, :, member] = np.transpose(one, (0, 2, 1, 3))
    y_matrix = y_block.reshape(4 * PAD, 4 * grid)
    cos_x, sin_x = pair(ranked)
    x_block = np.zeros((2, PAD, 2, grid, 2))
    for member in range(2):
        x_block[member, :, member] = np.stack([cos_x, sin_x], axis=-1)
    x_matrix = x_block.reshape(2 * PAD, 4 * grid)
    return [m.astype(ml_dtypes.bfloat16) for m in (z_matrix, y_matrix, x_matrix)]


def transform_kernel(
    grid, offsets, packed, val_ref, cond_ref, z_ref, y_ref, x_ref, out_ref, mid, cols
):
    half = 2 * PAD * 2
    lane = lax.broadcasted_iota(jnp.int32, (2 * grid, 2 * grid), 1)
    low = lane < grid

    def planes(step, carry):
        val = val_ref[0, pl.ds(step * 2, 2)].reshape(2 * grid, 2 * grid).astype(jnp.float32)
        turned = pltpu.roll(val, grid, 1)
        val_re = jnp.where(low, val, turned)
        val_im = jnp.where(low, turned, -val)
        fields = []
        for band in range(4):
            cond = cond_ref[band, pl.ds(step * 2, 2)].reshape(2 * grid, 2 * grid)
            cond = cond.astype(jnp.float32)
            product = val_re * cond + val_im * pltpu.roll(cond, grid, 1)
            fields.append(product.astype(jnp.bfloat16))
        parts = []
        for first in (0, 2):
            both = jnp.concatenate(fields[first : first + 2], axis=1)
            parts.append(
                jnp.dot(both, z_ref[...], preferred_element_type=jnp.float32).astype(jnp.bfloat16)
            )
        stacked = []
        for plane in range(2):
            rows = slice(plane * grid, (plane + 1) * grid)
            for which in range(2):
                lanes = slice(which * half, (which + 1) * half)
                stacked.append(
                    jnp.concatenate([parts[0][rows, lanes], parts[1][rows, lanes]], axis=1)
                )
        stacked = jnp.concatenate(stacked, axis=0)
        found = jnp.dot(y_ref[...], stacked, preferred_element_type=jnp.float32)
        start = pl.multiple_of(step * 4 * PAD, 4 * PAD)
        for side in range(2):
            mid[side, pl.ds(start, 4 * PAD), :] = found[:, side * half : (side + 1) * half]
        return carry

    lax.fori_loop(0, grid // 2, planes, 0, unroll=4)
    cols[...] = jnp.zeros_like(cols)
    count = len(offsets) - 1
    for first in range(0, count, 2):
        rows = [
            jnp.concatenate(
                [
                    mid[side, pl.ds(first + member, 2 * grid, stride=PAD), :].astype(jnp.bfloat16)
                    for side in range(2)
                ],
                axis=1,
            )
            for member in range(2)
        ]
        found = jnp.dot(
            x_ref[...], jnp.concatenate(rows, axis=0), preferred_element_type=jnp.float32
        )
        for member in range(2):
            if first + member < count:
                start = offsets[first + member]
                cols[start : start + PAD, :] = found[member * PAD : (member + 1) * PAD]
    turned = cols[...].T
    for k in range(PAD):
        out_ref[k, 0:4, :] = turned[4 * k : 4 * k + 4]
        out_ref[k, 4:8, :] = turned[half + 4 * k : half + 4 * k + 4]


def pick_tile(count, rows, packed, held, col, sel):
    tile = col.shape[1]
    place = lax.broadcasted_iota(jnp.int32, (packed, tile), 0)
    chosen = jnp.where(place == col, 1.0, 0.0).astype(jnp.bfloat16)
    found = jnp.dot(held[...], chosen, preferred_element_type=jnp.float32)
    select = jnp.broadcast_to(sel, (rows, tile))
    total = jnp.zeros((rows, tile), jnp.float32)
    for k in range(count):
        total = total + jnp.where(select == k, found[k * rows : (k + 1) * rows], 0.0)
    return total.astype(jnp.bfloat16)


def gather_kernel(
    plan, field_ref, col_ref, sel_ref, weight_ref, all_ref, row_ref, scale_ref, held, stage,
    x_send, x_recv, x_local, send, recv, r_send, r_recv, r_local,
):
    count, rows, packed, n_band, n_col, chunks, width, tile, share, window = plan
    n_z = n_band // 4
    me = lax.axis_index("band")
    my_col = lax.axis_index("col")
    z, y, core = me // 4, me // 2 % 2, me % 2
    y_peer = z * 4 + (1 - y) * 2 + core
    core_peer = z * 4 + y * 2 + 1 - core
    span = chunks * width

    def remote(src, dst, send_sem, recv_sem, **target):
        return pltpu.make_async_remote_copy(
            src_ref=src,
            dst_ref=dst,
            send_sem=send_sem,
            recv_sem=recv_sem,
            device_id=target,
            device_id_type=pl.DeviceIdType.MESH,
        )

    def inside(value):
        return (value >= 0) & (value < n_z)

    barrier = pltpu.get_barrier_semaphore()

    def greet(**target):
        pl.semaphore_signal(
            barrier, inc=1, device_id=target, device_id_type=pl.DeviceIdType.MESH
        )

    for step in (1, -1):
        pl.when(inside(z + step))(functools.partial(greet, band=me + 4 * step))
    greet(band=y_peer)
    greet(band=core_peer)
    for p in range(1, n_col):
        greet(col=(my_col + p) % n_col)
    known = (z > 0).astype(jnp.int32) + (z < n_z - 1).astype(jnp.int32) + 1 + n_col
    pl.semaphore_wait(barrier, known)

    def lanes(j):
        return pl.ds(pl.multiple_of(j * width, 128), width)

    def block(slot, j):
        return all_ref.at[slot, :, :, lanes(j)]

    def relay(act, slot, j, kind, target):
        view = block(slot, j)
        copy = remote(view, view, send.at[j, kind, slot], recv.at[j, slot], band=target)
        getattr(copy, act)()

        @pl.when(j == 0)
        def _():
            view = scale_ref.at[slot]
            getattr(
                remote(
                    view, view, send.at[chunks, kind, slot], recv.at[chunks, slot], band=target
                ),
                act,
            )()

    def staged(j, owner):
        return stage.at[:, pl.ds(pl.multiple_of(owner * span + j * width, 128), width)]

    def across(j, p):
        peer = (my_col + p) % n_col
        return remote(
            staged(j, peer),
            all_ref.at[me, my_col, :, lanes(j)],
            x_send.at[j, p],
            x_recv.at[j, p],
            col=peer,
        )

    def across_scale(p):
        return remote(
            weight_ref,
            scale_ref.at[me, my_col],
            x_send.at[chunks, p],
            x_recv.at[chunks, p],
            col=(my_col + p) % n_col,
        )

    def own_scale():
        return pltpu.make_async_copy(weight_ref, scale_ref.at[me, my_col], x_local.at[chunks])

    def own(j):
        return pltpu.make_async_copy(
            staged(j, my_col), all_ref.at[me, my_col, :, lanes(j)], x_local.at[j]
        )

    def pick(j):
        per = width // tile

        def body(i, carry):
            start = pl.multiple_of((i // per) * span + j * width + (i % per) * tile, 128)
            where = pl.ds(start, tile)
            stage[:, where] = pick_tile(
                count, rows, packed, held, col_ref[:, where], sel_ref[:, where]
            )
            return carry

        lax.fori_loop(0, n_col * per, body, 0)
        own(j).start()
        for p in range(1, n_col):
            across(j, p).start()

    def along_z(j, h, act):
        if h == 0 and act == "start":
            own(j).wait()
            for p in range(1, n_col):
                across(j, p).wait_recv()

            @pl.when(j == 0)
            def _():
                for p in range(1, n_col):
                    across_scale(p).wait_recv()

        for step in (1, -1):
            source = z - step * h
            slot = source * 4 + y * 2 + core

            @pl.when(inside(source))
            def _():
                if h > 0 and act == "start":
                    relay("wait_recv", slot, j, 2, y_peer)

                @pl.when(inside(z + step))
                def _():
                    relay(act, slot, j, 0 if step == 1 else 1, me + 4 * step)

                if h > 0 or step == 1:
                    relay(act, slot, j, 2, y_peer)
                    relay(act, slot, j, 3, core_peer)

    def along_y(j, h, act):
        for step in (1, -1) if h > 0 else (1,):
            source = z - step * h
            slot = source * 4 + (1 - y) * 2 + core

            @pl.when(inside(source))
            def _():
                if act == "start":
                    relay("wait_recv", slot, j, 3, core_peer)
                relay(act, slot, j, 3, core_peer)

    per_col = n_band // n_col
    owner = me // per_col
    base = me % per_col * share // 128 * 128

    def row_copy(i, p):
        return remote(
            all_ref.at[:, :, :, pl.ds(pl.multiple_of(base + 128 * i, 128), 128)],
            row_ref.at[:, :, :, pl.ds(128 * i, 128)],
            r_send.at[i, p],
            r_recv.at[i],
            col=(my_col + p) % n_col,
        )

    def row_local(i):
        return pltpu.make_async_copy(
            all_ref.at[:, :, :, pl.ds(pl.multiple_of(base + 128 * i, 128), 128)],
            row_ref.at[:, :, :, pl.ds(128 * i, 128)],
            r_local.at[i],
        )

    def finish(j):
        for other in range(2 * n_z):
            slot = other * 2 + 1 - core
            relay("wait_recv", slot, j, 3, core_peer)
        for i in range(window // 128):

            @pl.when((owner == my_col) & ((base + 128 * i) // width == j))
            def _():
                row_local(i).start()
                for p in range(1, n_col):
                    row_copy(i, p).start()

    own_scale().start()
    for p in range(1, n_col):
        across_scale(p).start()
    own_scale().wait()
    held[...] = field_ref[0:count].reshape(count * rows, packed).astype(jnp.bfloat16)

    def tick(t, carry):
        def at(lag, act):
            j = t - lag
            pl.when((j >= 0) & (j < chunks))(lambda: act(j))

        at(0, pick)
        at(n_z + 2, finish)
        for h in range(n_z - 1, -1, -1):
            at(2 + h, lambda j: along_y(j, h, "start"))
            at(1 + h, lambda j: along_z(j, h, "start"))
        return carry

    lax.fori_loop(0, chunks + n_z + 2, tick, 0)

    def settle(j, carry):
        for p in range(1, n_col):
            across(j, p).wait_send()
        for h in range(n_z):
            along_z(j, h, "wait_send")
            along_y(j, h, "wait_send")
        return carry

    lax.fori_loop(0, chunks, settle, 0)
    for p in range(1, n_col):
        across_scale(p).wait_send()
    for i in range(window // 128):

        @pl.when(owner == my_col)
        def _():
            row_local(i).wait()
            for p in range(1, n_col):
                row_copy(i, p).wait_send()

        @pl.when(owner != my_col)
        def _():
            row_copy(i, 1).wait_recv()


def densities(valence, conduction, gvec_index):
    val_local, grid = valence.shape[0], valence.shape[1]
    npw = gvec_index.shape[0]
    reach, offsets = sphere(grid, npw)
    count = 2 * reach + 1
    assert count <= PAD and conduction.shape[0] == 4
    packed = -(-(offsets[-2] + PAD) // 128) * 128
    z_matrix, y_matrix, x_matrix = tables(grid, reach)
    features = 8 * val_local
    whole = lambda shape: pl.BlockSpec(shape, lambda v: (0,) * len(shape))
    field = pl.pallas_call(
        functools.partial(transform_kernel, grid, offsets, packed),
        grid=(val_local,),
        in_specs=[
            pl.BlockSpec((1, grid, grid, 2 * grid), lambda v: (v, 0, 0, 0)),
            whole(conduction.shape),
            whole(z_matrix.shape),
            whole(y_matrix.shape),
            whole(x_matrix.shape),
        ],
        out_specs=pl.BlockSpec((PAD, 8, packed), lambda v: (0, v, 0)),
        out_shape=jax.ShapeDtypeStruct((PAD, features, packed), jnp.float32),
        scratch_shapes=[
            pltpu.VMEM((2, 2 * grid * PAD, 4 * PAD), jnp.float32),
            pltpu.VMEM((packed, 8 * PAD), jnp.float32),
        ],
        compiler_params=pltpu.CompilerParams(vmem_limit_bytes=VMEM),
        name="transform",
    )(valence, conduction, z_matrix, y_matrix, x_matrix)

    half = grid // 2
    wrap = lambda part: (part + half) % grid - half
    x_comp = wrap(gvec_index // (grid * grid))
    y_comp = wrap(gvec_index // grid % grid)
    z_comp = wrap(gvec_index % grid)
    col = jnp.where(x_comp > 0, 2 * x_comp - 1, -2 * x_comp)
    for k in range(count):
        col = col + jnp.where(y_comp == k - reach, offsets[k], 0)
    return field, col[None], (z_comp + reach)[None], count, packed


def gathered(weight, field, col, sel, count, packed):
    features, npw = field.shape[1], col.shape[1]
    n_band, n_col = lax.axis_size("band"), lax.axis_size("col")
    chunks = 5
    width = npw // n_col // chunks
    tile = min(512, width)
    share = npw // n_band
    window = -(-share // 128) * 128
    assert window >= share + max(share * r % 128 for r in range(n_band // n_col))
    plan = (count, features, packed, n_band, n_col, chunks, width, tile, share, window)
    vmem = pl.BlockSpec(memory_space=pltpu.VMEM)
    dma = pltpu.SemaphoreType.DMA
    pieces = window // 128
    cols, rows, scale = pl.pallas_call(
        functools.partial(gather_kernel, plan),
        in_specs=[vmem] * 4,
        out_specs=[pl.BlockSpec(memory_space=pl.ANY)] * 3,
        out_shape=[
            jax.ShapeDtypeStruct((n_band, n_col, features, chunks * width), jnp.bfloat16),
            jax.ShapeDtypeStruct((n_band, n_col, features, window), jnp.bfloat16),
            jax.ShapeDtypeStruct((n_band, n_col, 8, 128), jnp.float32),
        ],
        scratch_shapes=[
            pltpu.VMEM((count * features, packed), jnp.bfloat16),
            pltpu.VMEM((features, npw), jnp.bfloat16),
            dma((chunks + 1, n_col)),
            dma((chunks + 1, n_col)),
            dma((chunks + 1,)),
            dma((chunks + 1, 4, n_band)),
            dma((chunks + 1, n_band)),
            dma((pieces, n_col)),
            dma((pieces,)),
            dma((pieces,)),
        ],
        compiler_params=pltpu.CompilerParams(
            vmem_limit_bytes=VMEM, collective_id=0, has_side_effects=True
        ),
        name="pick_and_gather",
    )(field, col, sel, jnp.zeros((8, 128), jnp.float32).at[0, :features].set(weight))
    if share % 128:
        start = lax.axis_index("band") % (n_band // n_col) * share % 128
        rows = lax.dynamic_slice_in_dim(rows, start, share, axis=3)
    return cols, rows, scale[:, :, 0, :features].reshape(1, -1)


def pair_weights(energy_valence, energy_conduction, occ_valence, occ_conduction):
    total_val = energy_valence.shape[0] * lax.axis_size("col")
    total_cond = energy_conduction.shape[0] * lax.axis_size("band")
    occ_diff = (occ_valence[:, None] - occ_conduction[None, :]).astype(jnp.float32)
    return (
        occ_diff
        / (energy_valence[:, None] - energy_conduction[None, :])
        / math.sqrt(total_val * total_cond)
    )


def contract_kernel(share, row_ref, scale_ref, col_ref, out_ref, left):
    @pl.when(pl.program_id(0) == 0)
    def _():
        rows = (row_ref[...].astype(jnp.float32).T * scale_ref[...]).astype(jnp.bfloat16)
        left[0:share] = rows
        wide = rows.astype(jnp.float32)
        depth = wide.shape[1]
        even = lax.broadcasted_iota(jnp.int32, wide.shape, 1) % 2 == 0
        turned = jnp.where(even, pltpu.roll(wide, depth - 1, 1), -pltpu.roll(wide, 1, 1))
        left[share : 2 * share] = turned.astype(jnp.bfloat16)

    for part in range(2):
        out_ref[part] = jnp.dot(
            left[part * share : (part + 1) * share],
            col_ref[...],
            preferred_element_type=jnp.float32,
        )


def local(
    valence, conduction, energy_valence, energy_conduction, occ_valence, occ_conduction, gvec_index
):
    weight = pair_weights(energy_valence, energy_conduction, occ_valence, occ_conduction)
    weight = jnp.repeat(weight.reshape(-1), 2)
    cols, rows, scale = gathered(weight, *densities(valence, conduction, gvec_index))
    n_band, n_col, features, share = rows.shape
    depth, span = n_band * n_col * features, cols.shape[3]
    tile = 512 if span % 512 == 0 else 256
    return pl.pallas_call(
        functools.partial(contract_kernel, share),
        grid=(span // tile,),
        in_specs=[
            pl.BlockSpec((depth, share), lambda h: (0, 0)),
            pl.BlockSpec((1, depth), lambda h: (0, 0)),
            pl.BlockSpec((depth, tile), lambda h: (0, h)),
        ],
        out_specs=pl.BlockSpec((2, share, tile), lambda h: (0, 0, h)),
        out_shape=jax.ShapeDtypeStruct((2, share, span), jnp.float32),
        scratch_shapes=[pltpu.VMEM((2 * share, depth), jnp.bfloat16)],
        compiler_params=pltpu.CompilerParams(vmem_limit_bytes=VMEM),
        name="contract",
    )(rows.reshape(depth, share), scale, cols.reshape(depth, span))


def solution(mesh):
    return jax.shard_map(
        local,
        mesh=mesh,
        in_specs=(
            P("col", None, None, None),
            P("band", None, None, None),
            P("col"),
            P("band"),
            P("col"),
            P("band"),
            P(),
        ),
        out_specs=P(None, "band", "col"),
        check_vma=False,
    )
```

```python
import functools
import math

import jax
import jax.numpy as jnp
import ml_dtypes
import numpy as np
from jax import lax
from jax.experimental import pallas as pl
from jax.experimental.pallas import tpu as pltpu
from jax.sharding import PartitionSpec as P

PAD = 32
VMEM = 56 * 1024 * 1024


def sphere(grid, count):
    comp = (np.arange(grid) + grid // 2) % grid - grid // 2
    square = comp * comp
    lengths = square[:, None, None] + square[None, :, None] + square[None, None, :]
    top = int(np.sort(lengths.ravel())[count - 1])
    reach = math.isqrt(top)
    widths = [2 * math.isqrt(top - k * k) + 1 for k in range(-reach, reach + 1)]
    offsets = [0]
    for width in widths:
        offsets.append(offsets[-1] + width)
    return reach, offsets


def tables(grid, reach):
    freq = np.arange(PAD) - reach
    kept = (np.arange(PAD) < 2 * reach + 1).astype(np.float64)
    rank = np.arange(PAD)
    ranked = (rank + 1) // 2 * np.where(rank % 2 == 1, 1, -1)

    def pair(values):
        angle = 2.0 * math.pi / grid * ((values[:, None] * np.arange(grid)[None, :]) % grid)
        return (
            np.cos(angle) / math.sqrt(grid) * kept[:, None],
            np.sin(angle) / math.sqrt(grid) * kept[:, None],
        )

    cosine, sine = pair(freq)
    full = np.array([[cosine, sine], [-sine, cosine]])
    swapped = np.array([full[1], -full[0]])
    z_block = np.zeros((2, 2, grid, 2, PAD, 2, 2))
    for member in range(2):
        for which, part in enumerate((full, swapped)):
            z_block[member, :, :, which, :, member, :] = np.transpose(part, (1, 3, 2, 0))
    z_matrix = z_block.reshape(4 * grid, 8 * PAD)
    one = np.array([[cosine, sine], [-sine, cosine]])
    y_block = np.zeros((2, 2, PAD, 2, 2, grid))
    for member in range(2):
        y_block[member, :, :, member] = np.transpose(one, (0, 2, 1, 3))
    y_matrix = y_block.reshape(4 * PAD, 4 * grid)
    cos_x, sin_x = pair(ranked)
    x_block = np.zeros((2, PAD, 2, grid, 2))
    for member in range(2):
        x_block[member, :, member] = np.stack([cos_x, sin_x], axis=-1)
    x_matrix = x_block.reshape(2 * PAD, 4 * grid)
    return [m.astype(ml_dtypes.bfloat16) for m in (z_matrix, y_matrix, x_matrix)]


def transform_kernel(
    grid, offsets, packed, val_ref, cond_ref, z_ref, y_ref, x_ref, out_ref, mid, cols
):
    half = 2 * PAD * 2
    lane = lax.broadcasted_iota(jnp.int32, (2 * grid, 2 * grid), 1)
    low = lane < grid

    def planes(step, carry):
        val = val_ref[0, pl.ds(step * 2, 2)].reshape(2 * grid, 2 * grid).astype(jnp.float32)
        turned = pltpu.roll(val, grid, 1)
        val_re = jnp.where(low, val, turned)
        val_im = jnp.where(low, turned, -val)
        fields = []
        for band in range(4):
            cond = cond_ref[band, pl.ds(step * 2, 2)].reshape(2 * grid, 2 * grid)
            cond = cond.astype(jnp.float32)
            product = val_re * cond + val_im * pltpu.roll(cond, grid, 1)
            fields.append(product.astype(jnp.bfloat16))
        parts = []
        for first in (0, 2):
            both = jnp.concatenate(fields[first : first + 2], axis=1)
            parts.append(
                jnp.dot(both, z_ref[...], preferred_element_type=jnp.float32).astype(jnp.bfloat16)
            )
        stacked = []
        for plane in range(2):
            rows = slice(plane * grid, (plane + 1) * grid)
            for which in range(2):
                lanes = slice(which * half, (which + 1) * half)
                stacked.append(
                    jnp.concatenate([parts[0][rows, lanes], parts[1][rows, lanes]], axis=1)
                )
        stacked = jnp.concatenate(stacked, axis=0)
        found = jnp.dot(y_ref[...], stacked, preferred_element_type=jnp.float32)
        start = pl.multiple_of(step * 4 * PAD, 4 * PAD)
        for side in range(2):
            mid[side, pl.ds(start, 4 * PAD), :] = found[:, side * half : (side + 1) * half]
        return carry

    lax.fori_loop(0, grid // 2, planes, 0, unroll=4)
    cols[...] = jnp.zeros_like(cols)
    count = len(offsets) - 1
    for first in range(0, count, 2):
        rows = [
            jnp.concatenate(
                [
                    mid[side, pl.ds(first + member, 2 * grid, stride=PAD), :].astype(jnp.bfloat16)
                    for side in range(2)
                ],
                axis=1,
            )
            for member in range(2)
        ]
        found = jnp.dot(
            x_ref[...], jnp.concatenate(rows, axis=0), preferred_element_type=jnp.float32
        )
        for member in range(2):
            if first + member < count:
                start = offsets[first + member]
                cols[start : start + PAD, :] = found[member * PAD : (member + 1) * PAD]
    turned = cols[...].T
    for k in range(PAD):
        out_ref[k, 0:4, :] = turned[4 * k : 4 * k + 4]
        out_ref[k, 4:8, :] = turned[half + 4 * k : half + 4 * k + 4]


def pick_tile(count, rows, packed, held, col, sel):
    tile = col.shape[1]
    place = lax.broadcasted_iota(jnp.int32, (packed, tile), 0)
    chosen = jnp.where(place == col, 1.0, 0.0).astype(jnp.bfloat16)
    found = jnp.dot(held[...], chosen, preferred_element_type=jnp.float32)
    select = jnp.broadcast_to(sel, (rows, tile))
    total = jnp.zeros((rows, tile), jnp.float32)
    for k in range(count):
        total = total + jnp.where(select == k, found[k * rows : (k + 1) * rows], 0.0)
    return total.astype(jnp.bfloat16)


def gather_kernel(
    plan, field_ref, col_ref, sel_ref, weight_ref, all_ref, row_ref, scale_ref, held, stage,
    x_send, x_recv, x_local, send, recv, r_send, r_recv, r_local,
):
    count, rows, packed, n_band, n_col, chunks, groups, share, window = plan
    n_z = n_band // 4
    me = lax.axis_index("band")
    my_col = lax.axis_index("col")
    z, y, core = me // 4, me // 2 % 2, me % 2
    y_peer = z * 4 + (1 - y) * 2 + core
    core_peer = z * 4 + y * 2 + 1 - core
    group = chunks * 128

    def remote(src, dst, send_sem, recv_sem, **target):
        return pltpu.make_async_remote_copy(
            src_ref=src,
            dst_ref=dst,
            send_sem=send_sem,
            recv_sem=recv_sem,
            device_id=target,
            device_id_type=pl.DeviceIdType.MESH,
        )

    def inside(value):
        return (value >= 0) & (value < n_z)

    barrier = pltpu.get_barrier_semaphore()

    def greet(**target):
        pl.semaphore_signal(
            barrier, inc=1, device_id=target, device_id_type=pl.DeviceIdType.MESH
        )

    for step in (1, -1):
        pl.when(inside(z + step))(functools.partial(greet, band=me + 4 * step))
    greet(band=y_peer)
    greet(band=core_peer)
    for p in range(1, n_col):
        greet(col=(my_col + p) % n_col)
    known = (z > 0).astype(jnp.int32) + (z < n_z - 1).astype(jnp.int32) + 1 + n_col
    pl.semaphore_wait(barrier, known)

    def lanes(j):
        return pl.ds(pl.multiple_of(j * 128, 128), 128)

    def block(slot, j):
        return all_ref.at[slot, :, :, :, lanes(j)]

    def relay(act, slot, j, kind, target):
        view = block(slot, j)
        copy = remote(view, view, send.at[j, kind, slot], recv.at[j, slot], band=target)
        getattr(copy, act)()

        @pl.when(j == 0)
        def _():
            view = scale_ref.at[slot]
            getattr(
                remote(
                    view, view, send.at[chunks, kind, slot], recv.at[chunks, slot], band=target
                ),
                act,
            )()

    def staged(j, owner):
        return stage.at[j, owner]

    def across(j, p):
        peer = (my_col + p) % n_col
        return remote(
            staged(j, peer),
            all_ref.at[me, my_col, :, :, lanes(j)],
            x_send.at[j, p],
            x_recv.at[j, p],
            col=peer,
        )

    def across_scale(p):
        return remote(
            weight_ref,
            scale_ref.at[me, my_col],
            x_send.at[chunks, p],
            x_recv.at[chunks, p],
            col=(my_col + p) % n_col,
        )

    def own_scale():
        return pltpu.make_async_copy(weight_ref, scale_ref.at[me, my_col], x_local.at[chunks])

    def own(j):
        return pltpu.make_async_copy(
            staged(j, my_col), all_ref.at[me, my_col, :, :, lanes(j)], x_local.at[j]
        )

    def pick(j):
        pieces = min(4, groups)

        def body(i, carry):
            first = i * pieces
            start = (j * n_col * groups + first) * 128
            where = pl.ds(pl.multiple_of(start, 128), pieces * 128)
            found = pick_tile(count, rows, packed, held, col_ref[:, where], sel_ref[:, where])
            for k in range(pieces):
                stage[j, first // groups, first % groups + k] = found[:, k * 128 : (k + 1) * 128]
            return carry

        lax.fori_loop(0, n_col * groups // pieces, body, 0)
        own(j).start()
        for p in range(1, n_col):
            across(j, p).start()

    def along_z(j, h, act):
        if h == 0 and act == "start":
            own(j).wait()
            for p in range(1, n_col):
                across(j, p).wait_recv()

            @pl.when(j == 0)
            def _():
                for p in range(1, n_col):
                    across_scale(p).wait_recv()

        for step in (1, -1):
            source = z - step * h
            slot = source * 4 + y * 2 + core

            @pl.when(inside(source))
            def _():
                if h > 0 and act == "start":
                    relay("wait_recv", slot, j, 2, y_peer)

                @pl.when(inside(z + step))
                def _():
                    relay(act, slot, j, 0 if step == 1 else 1, me + 4 * step)

                if h > 0 or step == 1:
                    relay(act, slot, j, 2, y_peer)
                    relay(act, slot, j, 3, core_peer)

    def along_y(j, h, act):
        for step in (1, -1) if h > 0 else (1,):
            source = z - step * h
            slot = source * 4 + (1 - y) * 2 + core

            @pl.when(inside(source))
            def _():
                if act == "start":
                    relay("wait_recv", slot, j, 3, core_peer)
                relay(act, slot, j, 3, core_peer)

    per_col = n_band // n_col
    owner = me // per_col
    base = me % per_col * share // 128 * 128
    home, first_piece = base // group, base % group // 128

    def row_copy(i, p):
        return remote(
            all_ref.at[:, :, home, :, lanes(first_piece + i)],
            row_ref.at[:, :, :, pl.ds(128 * i, 128)],
            r_send.at[i, p],
            r_recv.at[i],
            col=(my_col + p) % n_col,
        )

    def row_local(i):
        return pltpu.make_async_copy(
            all_ref.at[:, :, home, :, lanes(first_piece + i)],
            row_ref.at[:, :, :, pl.ds(128 * i, 128)],
            r_local.at[i],
        )

    def finish(j):
        for other in range(2 * n_z):
            slot = other * 2 + 1 - core
            relay("wait_recv", slot, j, 3, core_peer)
        for i in range(window // 128):

            @pl.when((owner == my_col) & (first_piece + i == j))
            def _():
                row_local(i).start()
                for p in range(1, n_col):
                    row_copy(i, p).start()

    own_scale().start()
    for p in range(1, n_col):
        across_scale(p).start()
    own_scale().wait()
    held[...] = field_ref[0:count].reshape(count * rows, packed).astype(jnp.bfloat16)

    def tick(t, carry):
        def at(lag, act):
            j = t - lag
            pl.when((j >= 0) & (j < chunks))(lambda: act(j))

        at(0, pick)
        at(n_z + 2, finish)
        for h in range(n_z - 1, -1, -1):
            at(2 + h, lambda j: along_y(j, h, "start"))
            at(1 + h, lambda j: along_z(j, h, "start"))
        return carry

    lax.fori_loop(0, chunks + n_z + 2, tick, 0)

    def settle(j, carry):
        for p in range(1, n_col):
            across(j, p).wait_send()
        for h in range(n_z):
            along_z(j, h, "wait_send")
            along_y(j, h, "wait_send")
        return carry

    lax.fori_loop(0, chunks, settle, 0)
    for p in range(1, n_col):
        across_scale(p).wait_send()
    for i in range(window // 128):

        @pl.when(owner == my_col)
        def _():
            row_local(i).wait()
            for p in range(1, n_col):
                row_copy(i, p).wait_send()

        @pl.when(owner != my_col)
        def _():
            row_copy(i, 1).wait_recv()


def densities(valence, conduction, gvec_index):
    val_local, grid = valence.shape[0], valence.shape[1]
    npw = gvec_index.shape[0]
    reach, offsets = sphere(grid, npw)
    count = 2 * reach + 1
    assert count <= PAD and conduction.shape[0] == 4
    packed = -(-(offsets[-2] + PAD) // 128) * 128
    z_matrix, y_matrix, x_matrix = tables(grid, reach)
    features = 8 * val_local
    whole = lambda shape: pl.BlockSpec(shape, lambda v: (0,) * len(shape))
    field = pl.pallas_call(
        functools.partial(transform_kernel, grid, offsets, packed),
        grid=(val_local,),
        in_specs=[
            pl.BlockSpec((1, grid, grid, 2 * grid), lambda v: (v, 0, 0, 0)),
            whole(conduction.shape),
            whole(z_matrix.shape),
            whole(y_matrix.shape),
            whole(x_matrix.shape),
        ],
        out_specs=pl.BlockSpec((PAD, 8, packed), lambda v: (0, v, 0)),
        out_shape=jax.ShapeDtypeStruct((PAD, features, packed), jnp.float32),
        scratch_shapes=[
            pltpu.VMEM((2, 2 * grid * PAD, 4 * PAD), jnp.float32),
            pltpu.VMEM((packed, 8 * PAD), jnp.float32),
        ],
        compiler_params=pltpu.CompilerParams(vmem_limit_bytes=VMEM),
        name="transform",
    )(valence, conduction, z_matrix, y_matrix, x_matrix)

    half = grid // 2
    wrap = lambda part: (part + half) % grid - half
    x_comp = wrap(gvec_index // (grid * grid))
    y_comp = wrap(gvec_index // grid % grid)
    z_comp = wrap(gvec_index % grid)
    col = jnp.where(x_comp > 0, 2 * x_comp - 1, -2 * x_comp)
    for k in range(count):
        col = col + jnp.where(y_comp == k - reach, offsets[k], 0)
    return field, col[None], (z_comp + reach)[None], count, packed


def gathered(weight, field, col, sel, count, packed):
    features, npw = field.shape[1], col.shape[1]
    n_band, n_col = lax.axis_size("band"), lax.axis_size("col")
    chunks = 5
    groups = npw // n_col // (chunks * 128)
    share = npw // n_band
    window = -(-share // 128) * 128
    assert window >= share + max(share * r % 128 for r in range(n_band // n_col))
    for r in range(n_band // n_col):
        assert share * r % (chunks * 128) // 128 * 128 + window <= chunks * 128
    plan = (count, features, packed, n_band, n_col, chunks, groups, share, window)

    def reorder(values):
        values = values.reshape(n_col, groups, chunks, 128)
        return jnp.transpose(values, (2, 0, 1, 3)).reshape(1, npw)

    vmem = pl.BlockSpec(memory_space=pltpu.VMEM)
    dma = pltpu.SemaphoreType.DMA
    pieces = window // 128
    cols, rows, scale = pl.pallas_call(
        functools.partial(gather_kernel, plan),
        in_specs=[vmem] * 4,
        out_specs=[pl.BlockSpec(memory_space=pl.ANY)] * 3,
        out_shape=[
            jax.ShapeDtypeStruct(
                (n_band, n_col, groups, features, chunks * 128), jnp.bfloat16
            ),
            jax.ShapeDtypeStruct((n_band, n_col, features, window), jnp.bfloat16),
            jax.ShapeDtypeStruct((n_band, n_col, 8, 128), jnp.float32),
        ],
        scratch_shapes=[
            pltpu.VMEM((count * features, packed), jnp.bfloat16),
            pltpu.VMEM((chunks, n_col, groups, features, 128), jnp.bfloat16),
            dma((chunks + 1, n_col)),
            dma((chunks + 1, n_col)),
            dma((chunks + 1,)),
            dma((chunks + 1, 4, n_band)),
            dma((chunks + 1, n_band)),
            dma((pieces, n_col)),
            dma((pieces,)),
            dma((pieces,)),
        ],
        compiler_params=pltpu.CompilerParams(
            vmem_limit_bytes=VMEM, collective_id=0, has_side_effects=True
        ),
        name="pick_and_gather",
    )(field, reorder(col), reorder(sel), jnp.zeros((8, 128), jnp.float32).at[0, :features].set(weight))
    if share % 128:
        start = lax.axis_index("band") % (n_band // n_col) * share % 128
        rows = lax.dynamic_slice_in_dim(rows, start, share, axis=3)
    return cols, rows, scale[:, :, 0, :features].reshape(1, -1)


def pair_weights(energy_valence, energy_conduction, occ_valence, occ_conduction):
    total_val = energy_valence.shape[0] * lax.axis_size("col")
    total_cond = energy_conduction.shape[0] * lax.axis_size("band")
    occ_diff = (occ_valence[:, None] - occ_conduction[None, :]).astype(jnp.float32)
    return (
        occ_diff
        / (energy_valence[:, None] - energy_conduction[None, :])
        / math.sqrt(total_val * total_cond)
    )


def contract_kernel(share, row_ref, scale_ref, col_ref, out_ref, left):
    @pl.when(pl.program_id(0) == 0)
    def _():
        rows = (row_ref[...].astype(jnp.float32).T * scale_ref[...]).astype(jnp.bfloat16)
        left[0:share] = rows
        wide = rows.astype(jnp.float32)
        depth = wide.shape[1]
        even = lax.broadcasted_iota(jnp.int32, wide.shape, 1) % 2 == 0
        turned = jnp.where(even, pltpu.roll(wide, depth - 1, 1), -pltpu.roll(wide, 1, 1))
        left[share : 2 * share] = turned.astype(jnp.bfloat16)

    cols = col_ref[...]
    if cols.shape[3] % 16:
        cols = cols.astype(jnp.float32)
    cols = cols.reshape(left.shape[1], cols.shape[4]).astype(jnp.bfloat16)
    for part in range(2):
        out_ref[part] = jnp.dot(
            left[part * share : (part + 1) * share],
            cols,
            preferred_element_type=jnp.float32,
        )


def local(
    valence, conduction, energy_valence, energy_conduction, occ_valence, occ_conduction, gvec_index
):
    weight = pair_weights(energy_valence, energy_conduction, occ_valence, occ_conduction)
    weight = jnp.repeat(weight.reshape(-1), 2)
    cols, rows, scale = gathered(weight, *densities(valence, conduction, gvec_index))
    n_band, n_col, features, share = rows.shape
    depth, groups, tile = n_band * n_col * features, cols.shape[2], cols.shape[4]
    return pl.pallas_call(
        functools.partial(contract_kernel, share),
        grid=(groups,),
        in_specs=[
            pl.BlockSpec((depth, share), lambda h: (0, 0)),
            pl.BlockSpec((1, depth), lambda h: (0, 0)),
            pl.BlockSpec((n_band, n_col, 1, features, tile), lambda h: (0, 0, h, 0, 0)),
        ],
        out_specs=pl.BlockSpec((2, share, tile), lambda h: (0, 0, h)),
        out_shape=jax.ShapeDtypeStruct((2, share, groups * tile), jnp.float32),
        scratch_shapes=[pltpu.VMEM((2 * share, depth), jnp.bfloat16)],
        compiler_params=pltpu.CompilerParams(vmem_limit_bytes=VMEM),
        name="contract",
    )(rows.reshape(depth, share), scale, cols)


def solution(mesh):
    return jax.shard_map(
        local,
        mesh=mesh,
        in_specs=(
            P("col", None, None, None),
            P("band", None, None, None),
            P("col"),
            P("band"),
            P("col"),
            P("band"),
            P(),
        ),
        out_specs=P(None, "band", "col"),
        check_vma=False,
    )
```

```python
import functools
import math

import jax
import jax.numpy as jnp
import ml_dtypes
import numpy as np
from jax import lax
from jax.experimental import pallas as pl
from jax.experimental.pallas import tpu as pltpu
from jax.sharding import PartitionSpec as P

PAD = 32
VMEM = 56 * 1024 * 1024


def sphere(grid, count):
    comp = (np.arange(grid) + grid // 2) % grid - grid // 2
    square = comp * comp
    lengths = square[:, None, None] + square[None, :, None] + square[None, None, :]
    top = int(np.sort(lengths.ravel())[count - 1])
    reach = math.isqrt(top)
    widths = [2 * math.isqrt(top - k * k) + 1 for k in range(-reach, reach + 1)]
    offsets = [0]
    for width in widths:
        offsets.append(offsets[-1] + width)
    return reach, offsets


def tables(grid, reach):
    freq = np.arange(PAD) - reach
    kept = (np.arange(PAD) < 2 * reach + 1).astype(np.float64)
    rank = np.arange(PAD)
    ranked = (rank + 1) // 2 * np.where(rank % 2 == 1, 1, -1)

    def pair(values):
        angle = 2.0 * math.pi / grid * ((values[:, None] * np.arange(grid)[None, :]) % grid)
        return (
            np.cos(angle) / math.sqrt(grid) * kept[:, None],
            np.sin(angle) / math.sqrt(grid) * kept[:, None],
        )

    cosine, sine = pair(freq)
    full = np.array([[cosine, sine], [-sine, cosine]])
    swapped = np.array([full[1], -full[0]])
    z_block = np.zeros((2, 2, grid, 2, PAD, 2, 2))
    for member in range(2):
        for which, part in enumerate((full, swapped)):
            z_block[member, :, :, which, :, member, :] = np.transpose(part, (1, 3, 2, 0))
    z_matrix = z_block.reshape(4 * grid, 8 * PAD)
    one = np.array([[cosine, sine], [-sine, cosine]])
    y_block = np.zeros((2, 2, PAD, 2, 2, grid))
    for member in range(2):
        y_block[member, :, :, member] = np.transpose(one, (0, 2, 1, 3))
    y_matrix = y_block.reshape(4 * PAD, 4 * grid)
    cos_x, sin_x = pair(ranked)
    x_block = np.zeros((2, PAD, 2, grid, 2))
    for member in range(2):
        x_block[member, :, member] = np.stack([cos_x, sin_x], axis=-1)
    x_matrix = x_block.reshape(2 * PAD, 4 * grid)
    return [m.astype(ml_dtypes.bfloat16) for m in (z_matrix, y_matrix, x_matrix)]


def transform_kernel(
    grid, offsets, packed, val_ref, cond_ref, z_ref, y_ref, x_ref, out_ref, mid, cols
):
    half = 2 * PAD * 2
    lane = lax.broadcasted_iota(jnp.int32, (2 * grid, 2 * grid), 1)
    low = lane < grid

    def planes(step, carry):
        val = val_ref[0, pl.ds(step * 2, 2)].reshape(2 * grid, 2 * grid).astype(jnp.float32)
        turned = pltpu.roll(val, grid, 1)
        val_re = jnp.where(low, val, turned)
        val_im = jnp.where(low, turned, -val)
        fields = []
        for band in range(4):
            cond = cond_ref[band, pl.ds(step * 2, 2)].reshape(2 * grid, 2 * grid)
            cond = cond.astype(jnp.float32)
            product = val_re * cond + val_im * pltpu.roll(cond, grid, 1)
            fields.append(product.astype(jnp.bfloat16))
        parts = []
        for first in (0, 2):
            both = jnp.concatenate(fields[first : first + 2], axis=1)
            parts.append(
                jnp.dot(both, z_ref[...], preferred_element_type=jnp.float32).astype(jnp.bfloat16)
            )
        stacked = []
        for plane in range(2):
            rows = slice(plane * grid, (plane + 1) * grid)
            for which in range(2):
                lanes = slice(which * half, (which + 1) * half)
                stacked.append(
                    jnp.concatenate([parts[0][rows, lanes], parts[1][rows, lanes]], axis=1)
                )
        stacked = jnp.concatenate(stacked, axis=0)
        found = jnp.dot(y_ref[...], stacked, preferred_element_type=jnp.float32)
        start = pl.multiple_of(step * 4 * PAD, 4 * PAD)
        for side in range(2):
            mid[side, pl.ds(start, 4 * PAD), :] = found[:, side * half : (side + 1) * half]
        return carry

    lax.fori_loop(0, grid // 2, planes, 0, unroll=8)
    cols[...] = jnp.zeros_like(cols)
    count = len(offsets) - 1
    for first in range(0, count, 2):
        rows = [
            jnp.concatenate(
                [
                    mid[side, pl.ds(first + member, 2 * grid, stride=PAD), :].astype(jnp.bfloat16)
                    for side in range(2)
                ],
                axis=1,
            )
            for member in range(2)
        ]
        found = jnp.dot(
            x_ref[...], jnp.concatenate(rows, axis=0), preferred_element_type=jnp.float32
        )
        for member in range(2):
            if first + member < count:
                start = offsets[first + member]
                cols[start : start + PAD, :] = found[member * PAD : (member + 1) * PAD]
    turned = cols[...].T
    for k in range(PAD):
        out_ref[k, 0:4, :] = turned[4 * k : 4 * k + 4]
        out_ref[k, 4:8, :] = turned[half + 4 * k : half + 4 * k + 4]


def pick_tile(count, rows, packed, held, col, sel):
    tile = col.shape[1]
    place = lax.broadcasted_iota(jnp.int32, (packed, tile), 0)
    chosen = jnp.where(place == col, 1.0, 0.0).astype(jnp.bfloat16)
    found = jnp.dot(held[...], chosen, preferred_element_type=jnp.float32)
    select = jnp.broadcast_to(sel, (rows, tile))
    total = jnp.zeros((rows, tile), jnp.float32)
    for k in range(count):
        total = total + jnp.where(select == k, found[k * rows : (k + 1) * rows], 0.0)
    return total.astype(jnp.bfloat16)


def gather_kernel(
    plan, field_ref, col_ref, sel_ref, weight_ref, all_ref, row_ref, scale_ref, held, stage,
    x_send, x_recv, x_local, send, recv, r_send, r_recv, r_local,
):
    count, rows, packed, n_band, n_col, chunks, groups, share, window = plan
    n_z = n_band // 4
    me = lax.axis_index("band")
    my_col = lax.axis_index("col")
    z, y, core = me // 4, me // 2 % 2, me % 2
    y_peer = z * 4 + (1 - y) * 2 + core
    core_peer = z * 4 + y * 2 + 1 - core
    group = chunks * 128

    def remote(src, dst, send_sem, recv_sem, **target):
        return pltpu.make_async_remote_copy(
            src_ref=src,
            dst_ref=dst,
            send_sem=send_sem,
            recv_sem=recv_sem,
            device_id=target,
            device_id_type=pl.DeviceIdType.MESH,
        )

    def inside(value):
        return (value >= 0) & (value < n_z)

    barrier = pltpu.get_barrier_semaphore()

    def greet(**target):
        pl.semaphore_signal(
            barrier, inc=1, device_id=target, device_id_type=pl.DeviceIdType.MESH
        )

    for step in (1, -1):
        pl.when(inside(z + step))(functools.partial(greet, band=me + 4 * step))
    greet(band=y_peer)
    greet(band=core_peer)
    for p in range(1, n_col):
        greet(col=(my_col + p) % n_col)
    known = (z > 0).astype(jnp.int32) + (z < n_z - 1).astype(jnp.int32) + 1 + n_col
    pl.semaphore_wait(barrier, known)

    def lanes(j):
        return pl.ds(pl.multiple_of(j * 128, 128), 128)

    def block(slot, j):
        return all_ref.at[slot, :, :, :, lanes(j)]

    def relay(act, slot, j, kind, target):
        view = block(slot, j)
        copy = remote(view, view, send.at[j, kind, slot], recv.at[j, slot], band=target)
        getattr(copy, act)()

        @pl.when(j == 0)
        def _():
            view = scale_ref.at[slot]
            getattr(
                remote(
                    view, view, send.at[chunks, kind, slot], recv.at[chunks, slot], band=target
                ),
                act,
            )()

    def staged(j, owner):
        return stage.at[j, owner]

    def across(j, p):
        peer = (my_col + p) % n_col
        return remote(
            staged(j, peer),
            all_ref.at[me, my_col, :, :, lanes(j)],
            x_send.at[j, p],
            x_recv.at[j, p],
            col=peer,
        )

    def across_scale(p):
        return remote(
            weight_ref,
            scale_ref.at[me, my_col],
            x_send.at[chunks, p],
            x_recv.at[chunks, p],
            col=(my_col + p) % n_col,
        )

    def own_scale():
        return pltpu.make_async_copy(weight_ref, scale_ref.at[me, my_col], x_local.at[chunks])

    def own(j):
        return pltpu.make_async_copy(
            staged(j, my_col), all_ref.at[me, my_col, :, :, lanes(j)], x_local.at[j]
        )

    def pick(j):
        pieces = min(4, groups)

        def body(i, carry):
            first = i * pieces
            start = (j * n_col * groups + first) * 128
            where = pl.ds(pl.multiple_of(start, 128), pieces * 128)
            found = pick_tile(count, rows, packed, held, col_ref[:, where], sel_ref[:, where])
            for k in range(pieces):
                stage[j, first // groups, first % groups + k] = found[:, k * 128 : (k + 1) * 128]
            return carry

        lax.fori_loop(0, n_col * groups // pieces, body, 0, unroll=2)
        own(j).start()
        for p in range(1, n_col):
            across(j, p).start()

    def along_z(j, h, act):
        if h == 0 and act == "start":
            own(j).wait()
            for p in range(1, n_col):
                across(j, p).wait_recv()

            @pl.when(j == 0)
            def _():
                for p in range(1, n_col):
                    across_scale(p).wait_recv()

        for step in (1, -1):
            source = z - step * h
            slot = source * 4 + y * 2 + core

            @pl.when(inside(source))
            def _():
                if h > 0 and act == "start":
                    relay("wait_recv", slot, j, 2, y_peer)

                @pl.when(inside(z + step))
                def _():
                    relay(act, slot, j, 0 if step == 1 else 1, me + 4 * step)

                if h > 0 or step == 1:
                    relay(act, slot, j, 2, y_peer)
                    relay(act, slot, j, 3, core_peer)

    def along_y(j, h, act):
        for step in (1, -1) if h > 0 else (1,):
            source = z - step * h
            slot = source * 4 + (1 - y) * 2 + core

            @pl.when(inside(source))
            def _():
                if act == "start":
                    relay("wait_recv", slot, j, 3, core_peer)
                relay(act, slot, j, 3, core_peer)

    per_col = n_band // n_col
    owner = me // per_col
    base = me % per_col * share // 128 * 128
    home, first_piece = base // group, base % group // 128

    def row_copy(i, p):
        return remote(
            all_ref.at[:, :, home, :, lanes(first_piece + i)],
            row_ref.at[:, :, :, pl.ds(128 * i, 128)],
            r_send.at[i, p],
            r_recv.at[i],
            col=(my_col + p) % n_col,
        )

    def row_local(i):
        return pltpu.make_async_copy(
            all_ref.at[:, :, home, :, lanes(first_piece + i)],
            row_ref.at[:, :, :, pl.ds(128 * i, 128)],
            r_local.at[i],
        )

    def finish(j):
        for other in range(2 * n_z):
            slot = other * 2 + 1 - core
            relay("wait_recv", slot, j, 3, core_peer)
        for i in range(window // 128):

            @pl.when((owner == my_col) & (first_piece + i == j))
            def _():
                row_local(i).start()
                for p in range(1, n_col):
                    row_copy(i, p).start()

    own_scale().start()
    for p in range(1, n_col):
        across_scale(p).start()
    own_scale().wait()
    held[...] = field_ref[0:count].reshape(count * rows, packed).astype(jnp.bfloat16)

    def tick(t, carry):
        def at(lag, act):
            j = t - lag
            pl.when((j >= 0) & (j < chunks))(lambda: act(j))

        at(0, pick)
        for h in range(n_z):
            at(1 + h, lambda j: along_z(j, h, "start"))
        for h in range(n_z):
            at(2 + h, lambda j: along_y(j, h, "start"))
        at(n_z + 2, finish)
        return carry

    lax.fori_loop(0, chunks + n_z + 2, tick, 0)

    def settle(j, carry):
        for p in range(1, n_col):
            across(j, p).wait_send()
        for h in range(n_z):
            along_z(j, h, "wait_send")
            along_y(j, h, "wait_send")
        return carry

    lax.fori_loop(0, chunks, settle, 0)
    for p in range(1, n_col):
        across_scale(p).wait_send()
    for i in range(window // 128):

        @pl.when(owner == my_col)
        def _():
            row_local(i).wait()
            for p in range(1, n_col):
                row_copy(i, p).wait_send()

        @pl.when(owner != my_col)
        def _():
            row_copy(i, 1).wait_recv()


def densities(valence, conduction, gvec_index):
    val_local, grid = valence.shape[0], valence.shape[1]
    npw = gvec_index.shape[0]
    reach, offsets = sphere(grid, npw)
    count = 2 * reach + 1
    assert count <= PAD and conduction.shape[0] == 4
    packed = -(-(offsets[-2] + PAD) // 128) * 128
    z_matrix, y_matrix, x_matrix = tables(grid, reach)
    features = 8 * val_local
    whole = lambda shape: pl.BlockSpec(shape, lambda v: (0,) * len(shape))
    field = pl.pallas_call(
        functools.partial(transform_kernel, grid, offsets, packed),
        grid=(val_local,),
        in_specs=[
            pl.BlockSpec((1, grid, grid, 2 * grid), lambda v: (v, 0, 0, 0)),
            whole(conduction.shape),
            whole(z_matrix.shape),
            whole(y_matrix.shape),
            whole(x_matrix.shape),
        ],
        out_specs=pl.BlockSpec((PAD, 8, packed), lambda v: (0, v, 0)),
        out_shape=jax.ShapeDtypeStruct((PAD, features, packed), jnp.float32),
        scratch_shapes=[
            pltpu.VMEM((2, 2 * grid * PAD, 4 * PAD), jnp.float32),
            pltpu.VMEM((packed, 8 * PAD), jnp.float32),
        ],
        compiler_params=pltpu.CompilerParams(vmem_limit_bytes=VMEM),
        name="transform",
    )(valence, conduction, z_matrix, y_matrix, x_matrix)

    half = grid // 2
    wrap = lambda part: (part + half) % grid - half
    x_comp = wrap(gvec_index // (grid * grid))
    y_comp = wrap(gvec_index // grid % grid)
    z_comp = wrap(gvec_index % grid)
    col = jnp.where(x_comp > 0, 2 * x_comp - 1, -2 * x_comp)
    for k in range(count):
        col = col + jnp.where(y_comp == k - reach, offsets[k], 0)
    return field, col[None], (z_comp + reach)[None], count, packed


def gathered(weight, field, col, sel, count, packed):
    features, npw = field.shape[1], col.shape[1]
    n_band, n_col = lax.axis_size("band"), lax.axis_size("col")
    chunks = 5
    groups = npw // n_col // (chunks * 128)
    share = npw // n_band
    window = -(-share // 128) * 128
    assert window >= share + max(share * r % 128 for r in range(n_band // n_col))
    for r in range(n_band // n_col):
        assert share * r % (chunks * 128) // 128 * 128 + window <= chunks * 128
    plan = (count, features, packed, n_band, n_col, chunks, groups, share, window)

    def reorder(values):
        values = values.reshape(n_col, groups, chunks, 128)
        return jnp.transpose(values, (2, 0, 1, 3)).reshape(1, npw)

    vmem = pl.BlockSpec(memory_space=pltpu.VMEM)
    dma = pltpu.SemaphoreType.DMA
    pieces = window // 128
    cols, rows, scale = pl.pallas_call(
        functools.partial(gather_kernel, plan),
        in_specs=[vmem] * 4,
        out_specs=[pl.BlockSpec(memory_space=pl.ANY)] * 3,
        out_shape=[
            jax.ShapeDtypeStruct(
                (n_band, n_col, groups, features, chunks * 128), jnp.bfloat16
            ),
            jax.ShapeDtypeStruct((n_band, n_col, features, window), jnp.bfloat16),
            jax.ShapeDtypeStruct((n_band, n_col, 8, 128), jnp.float32),
        ],
        scratch_shapes=[
            pltpu.VMEM((count * features, packed), jnp.bfloat16),
            pltpu.VMEM((chunks, n_col, groups, features, 128), jnp.bfloat16),
            dma((chunks + 1, n_col)),
            dma((chunks + 1, n_col)),
            dma((chunks + 1,)),
            dma((chunks + 1, 4, n_band)),
            dma((chunks + 1, n_band)),
            dma((pieces, n_col)),
            dma((pieces,)),
            dma((pieces,)),
        ],
        compiler_params=pltpu.CompilerParams(
            vmem_limit_bytes=VMEM, collective_id=0, has_side_effects=True
        ),
        name="pick_and_gather",
    )(field, reorder(col), reorder(sel), jnp.zeros((8, 128), jnp.float32).at[0, :features].set(weight))
    if share % 128:
        start = lax.axis_index("band") % (n_band // n_col) * share % 128
        rows = lax.dynamic_slice_in_dim(rows, start, share, axis=3)
    return cols, rows, scale[:, :, 0, :features].reshape(1, -1)


def pair_weights(energy_valence, energy_conduction, occ_valence, occ_conduction):
    total_val = energy_valence.shape[0] * lax.axis_size("col")
    total_cond = energy_conduction.shape[0] * lax.axis_size("band")
    occ_diff = (occ_valence[:, None] - occ_conduction[None, :]).astype(jnp.float32)
    return (
        occ_diff
        / (energy_valence[:, None] - energy_conduction[None, :])
        / math.sqrt(total_val * total_cond)
    )


def contract_kernel(share, row_ref, scale_ref, col_ref, out_ref, left):
    @pl.when(pl.program_id(0) == 0)
    def _():
        rows = (row_ref[...].astype(jnp.float32).T * scale_ref[...]).astype(jnp.bfloat16)
        left[0:share] = rows
        wide = rows.astype(jnp.float32)
        depth = wide.shape[1]
        even = lax.broadcasted_iota(jnp.int32, wide.shape, 1) % 2 == 0
        turned = jnp.where(even, pltpu.roll(wide, depth - 1, 1), -pltpu.roll(wide, 1, 1))
        left[share : 2 * share] = turned.astype(jnp.bfloat16)

    cols = col_ref[...]
    if cols.shape[3] % 16:
        cols = cols.astype(jnp.float32)
    cols = cols.reshape(left.shape[1], cols.shape[4]).astype(jnp.bfloat16)
    for part in range(2):
        out_ref[part] = jnp.dot(
            left[part * share : (part + 1) * share],
            cols,
            preferred_element_type=jnp.float32,
        )


def local(
    valence, conduction, energy_valence, energy_conduction, occ_valence, occ_conduction, gvec_index
):
    weight = pair_weights(energy_valence, energy_conduction, occ_valence, occ_conduction)
    weight = jnp.repeat(weight.reshape(-1), 2)
    cols, rows, scale = gathered(weight, *densities(valence, conduction, gvec_index))
    n_band, n_col, features, share = rows.shape
    depth, groups, tile = n_band * n_col * features, cols.shape[2], cols.shape[4]
    return pl.pallas_call(
        functools.partial(contract_kernel, share),
        grid=(groups,),
        in_specs=[
            pl.BlockSpec((depth, share), lambda h: (0, 0)),
            pl.BlockSpec((1, depth), lambda h: (0, 0)),
            pl.BlockSpec((n_band, n_col, 1, features, tile), lambda h: (0, 0, h, 0, 0)),
        ],
        out_specs=pl.BlockSpec((2, share, tile), lambda h: (0, 0, h)),
        out_shape=jax.ShapeDtypeStruct((2, share, groups * tile), jnp.float32),
        scratch_shapes=[pltpu.VMEM((2 * share, depth), jnp.bfloat16)],
        compiler_params=pltpu.CompilerParams(vmem_limit_bytes=VMEM),
        name="contract",
    )(rows.reshape(depth, share), scale, cols)


def solution(mesh):
    return jax.shard_map(
        local,
        mesh=mesh,
        in_specs=(
            P("col", None, None, None),
            P("band", None, None, None),
            P("col"),
            P("band"),
            P("col"),
            P("band"),
            P(),
        ),
        out_specs=P(None, "band", "col"),
        check_vma=False,
    )
```
